32 devices in a mesh: groups: 2 (over y), rows: 8 (over z, x), layers: 2 (over core).
Axes of the slice: x: 2, y: 2, z: 4, core: 2. Of those that a mesh axis runs over, the one named last changes fastest.
Arguments:
- train_grads: bfloat16 [6144, 2, 4096], P(('groups', 'rows'), 'layers'), parts along dimension 0, may hold values from -6 to 6
- query_grads: bfloat16 [2, 2048, 4096], P('layers', ('groups', 'rows')), parts along dimension 1, may hold values from -0.09375 to 0.09375
Outputs:
- scores: float32 [1024, 6144], P('layers', ('groups', 'rows')), parts along dimension 1
The draws below stay inside these ranges and needn't reach their ends.
There are 2 independent parts, one for each index of `groups`. The reference program is written for one: setup_inputs(seed, part) draws one part's arguments, and reference() takes and returns one part's arrays. A program takes and returns all parts, laid end to end along the dimension named above; each array names one. Nothing has to cross between parts.
All inputs are finite; a program needn't handle non-finite values.
Results may differ from the reference program's by a relative error of at most 0.0003.
Values may be sent and summed in bfloat16 or wider, within the bound.
A program may use at most 64 MiB of HBM per device.

```python
import jax
import jax.numpy as jnp
from jax import lax

K = 4096
Q = 1024
L = 2
NTRAIN = 3072


def spiked(array, own_key, source, target, blocks, factor):
    owner, partner = [(jnp.arange(array.shape[dim]) // (array.shape[dim] // blocks)).reshape([-1 if axis == dim else 1 for axis in range(array.ndim)]) for dim in (source, target)]
    chosen = jax.random.permutation(own_key, blocks)[partner]
    strong = (owner == chosen) | (owner == (partner + blocks // 2) % blocks)
    return jnp.where(strong, factor * array, array)


def levels(key, shape, pieces, low, high):
    level = 1.0
    for dim, parts in pieces:
        steps = jax.random.uniform(jax.random.fold_in(jax.random.fold_in(key, 6), dim), (parts,), jnp.float32, low / len(pieces), high / len(pieces))
        level = level * jnp.repeat(jnp.exp(steps), shape[dim] // parts).reshape((-1,) + (1,) * (len(shape) - 1 - dim))
    return level


def normal_values(stream_key, shape, deviation, bound, cuts=(), kind=jnp.bfloat16):
    factor_of = levels(stream_key, shape, cuts, -0.22, 0.18) if cuts else 1.0
    array = jax.random.normal(stream_key, shape, jnp.float32) * deviation * factor_of
    return jnp.minimum(jnp.maximum(array, -bound), bound).astype(kind)


def bell_draw_with(own_key, extent, spread, most, pieces, heavy, held_as=jnp.bfloat16):
    result = spread * jax.random.normal(own_key, extent, jnp.float32)
    if pieces:
        result = result * levels(own_key, extent, pieces, -0.22, 0.18)
    return jnp.clip(spiked(result, jax.random.fold_in(own_key, 3), *heavy), -most, most).astype(held_as)


def setup_inputs(seed: int = 0, part: int = 0) -> dict:
    streams_of = jax.random.split(jax.random.key(seed), 3)
    own_keys = jax.random.split(jax.random.fold_in(streams_of[2], part), 3)
    return {
        "train_grads": normal_values(own_keys[0], (NTRAIN, L, K), 1.0, 6.0, ((0, 8), (1, 2))),
        "query_grads": bell_draw_with(own_keys[1], (L, Q, K), (K * L) ** -0.5, 0.09375, ((0, 2), (1, 8)), (0, 1, 2, 2.0)),
    }


def reference(train_grads, query_grads):
    def layer_step(total, index):
        block = lax.dynamic_index_in_dim(train_grads, index, 1, keepdims=False)
        queries = lax.dynamic_index_in_dim(query_grads, index, 0, keepdims=False)
        part = lax.dot_general(queries, block, (((1,), (1,)), ((), ())), preferred_element_type=jnp.float32)
        return total + part, None

    start = jnp.zeros((query_grads.shape[1], train_grads.shape[0]), jnp.float32)
    total, unused = lax.scan(layer_step, start, jnp.arange(train_grads.shape[1], dtype=jnp.int32))
    return total
```

```python
import functools
import math

import jax
import jax.numpy as jnp
from jax import lax
from jax.experimental import pallas as pl
from jax.experimental.pallas import tpu as pltpu
from jax.sharding import PartitionSpec as P

PARTS = 2
PIECES = 4
MESH = pl.DeviceIdType.MESH


def schedule(step, place, side, line, parts):
    subs = 2 * parts
    near = jnp.minimum(place, line - 1 - place)
    far = jnp.where(place < line - 1 - place, 1, -1)
    past = step - subs
    paired = past < 2 * near * subs
    within = lax.rem(past, 2 * subs)
    rest = past - 2 * near * subs
    apart = jnp.where(paired, past // (2 * subs) + 1, near + 1 + rest // subs)
    way = jnp.where(paired & (lax.rem(within, 2) == 1), -far, far)
    own = step < subs
    position = jnp.where(own, place, place + way * apart)
    turn = jnp.where(own, step, jnp.where(paired, within // 2, lax.rem(rest, subs)))
    shard = jnp.where(turn < parts, side, 1 - side)
    return position, shard, lax.rem(turn, parts)


def kernel(line, layers, parts, train, queries, out, qbuf, tbuf, pbuf, lbuf, rbuf,
           q_recv, q_send, x_send, t_recv, t_send, l_recv, l_send, r_recv, r_send):
    chunks, height, half = qbuf.shape
    rows = tbuf.shape[1]
    owned = rbuf.shape[0]
    subs = 2 * parts
    me = lax.axis_index("rows")
    layer = lax.axis_index("layers")
    place, side = me // 2, lax.rem(me, 2)
    other = 1 - side
    twin = me + 1 - 2 * side
    has_left, has_right = place > 0, place < line - 1
    left = jnp.where(has_left, me - 2, me)
    right = jnp.where(has_right, me + 2, me)
    pieces = t_recv.shape[0] - 1
    tall = rows // pieces
    mine = pl.ds(pl.multiple_of(side * half, half), half)
    theirs = pl.ds(pl.multiple_of(other * half, half), half)

    def name(position, shard, part):
        return (position * 2 + shard) * parts + part

    def visit(step):
        position, shard, part = schedule(step, place, side, line, parts)
        return position, name(position, shard, part)

    def remote(src, dst, send, recv, axis, device):
        return pltpu.make_async_remote_copy(
            src_ref=src, dst_ref=dst, send_sem=send, recv_sem=recv,
            device_id={axis: device}, device_id_type=MESH)

    def local_query(part):
        chunk = name(place, side, part)
        return pltpu.make_async_copy(
            queries.at[pl.ds(part * height, height), mine], qbuf.at[chunk], q_recv.at[chunk])

    def twin_query(part):
        chunk = name(place, side, part)
        return remote(queries.at[pl.ds(part * height, height), theirs], qbuf.at[chunk],
                      x_send.at[part], q_recv.at[chunk], "rows", twin)

    def own_query(part, way, device):
        chunk = name(place, side, part)
        return remote(queries.at[pl.ds(part * height, height), mine], qbuf.at[chunk],
                      q_send.at[way, chunk], q_recv.at[chunk], "rows", device)

    def forward(chunk, way, device):
        return remote(qbuf.at[chunk], qbuf.at[chunk], q_send.at[way, chunk], q_recv.at[chunk],
                      "rows", device)

    def twin_train(piece):
        return remote(train.at[pl.ds(piece * tall, tall), theirs],
                      tbuf.at[side, pl.ds(piece * tall, tall), :],
                      t_send.at[piece], t_recv.at[piece], "rows", twin)

    def local_train():
        return pltpu.make_async_copy(train.at[:, mine], tbuf.at[side], t_recv.at[pieces])

    def split(chunk):
        owner = chunk // owned
        return owner, chunk - owner * owned

    def to_layer(chunk):
        owner, index = split(chunk)
        return remote(pbuf.at[chunk], lbuf.at[layer, index], l_send.at[chunk],
                      l_recv.at[layer, index], "layers", owner)

    def to_twin(chunk):
        _, index = split(chunk)
        return remote(pbuf.at[chunk, other], rbuf.at[index], r_send.at[index], r_recv.at[index],
                      "rows", twin)

    barrier = pltpu.get_barrier_semaphore()
    pl.semaphore_signal(barrier, inc=1, device_id={"rows": twin}, device_id_type=MESH)

    @pl.when(has_left)
    def _():
        pl.semaphore_signal(barrier, inc=1, device_id={"rows": left}, device_id_type=MESH)

    @pl.when(has_right)
    def _():
        pl.semaphore_signal(barrier, inc=1, device_id={"rows": right}, device_id_type=MESH)

    for hop in range(1, layers):
        pl.semaphore_signal(barrier, inc=1, device_id={"layers": lax.rem(layer + hop, layers)},
                            device_id_type=MESH)
    for part in range(parts):
        local_query(part).start()
    local_train().start()
    pl.semaphore_wait(
        barrier, layers + has_left.astype(jnp.int32) + has_right.astype(jnp.int32))

    for part in range(parts):
        twin_query(part).start()

        @pl.when(has_left)
        def _():
            own_query(part, 0, left).start()

        @pl.when(has_right)
        def _():
            own_query(part, 1, right).start()

    def arrive(step):
        position, chunk = visit(step)
        own = step < parts
        forward(chunk, 0, twin).wait_recv()

        @pl.when((position >= place) & has_left & jnp.logical_not(own))
        def _():
            forward(chunk, 0, left).start()

        @pl.when((position <= place) & has_right & jnp.logical_not(own))
        def _():
            forward(chunk, 1, right).start()

    def loop(low, high, body):
        lax.fori_loop(low, high, lambda step, carry: (body(step), carry)[1], 0)

    loop(0, subs, arrive)
    for piece in range(pieces):
        twin_train(piece).start()
    early = jnp.where(has_left & has_right, chunks, chunks - subs)
    loop(subs, early, arrive)
    local_train().wait()
    for piece in range(pieces):
        remote(tbuf.at[other, pl.ds(piece * tall, tall), :], tbuf.at[other, pl.ds(piece * tall, tall), :],
               t_send.at[piece], t_recv.at[piece], "rows", twin).wait_recv()

    def product(step):
        @pl.when(step >= early)
        def _():
            arrive(step)

        _, chunk = visit(step)
        owner, _ = split(chunk)
        block = qbuf[chunk]
        for shard in range(2):
            pbuf[chunk, shard] = lax.dot_general(
                block, tbuf[shard], (((1,), (1,)), ((), ())), preferred_element_type=jnp.float32)

        @pl.when(owner != layer)
        def _():
            to_layer(chunk).start()

    def sum_layers(step):
        _, chunk = visit(step)
        owner, index = split(chunk)

        @pl.when(owner == layer)
        def _():
            for hop in range(1, layers):
                source = lax.rem(layer + hop, layers)
                remote(pbuf.at[chunk], lbuf.at[source, index], l_send.at[chunk],
                       l_recv.at[source, index], "rows", twin).wait_recv()
                for shard in range(2):
                    pbuf[chunk, shard] = pbuf[chunk, shard] + lbuf[source, index, shard]
            to_twin(chunk).start()

    def both(step):
        product(step)

        @pl.when(step > 0)
        def _():
            sum_layers(step - 1)

    loop(0, chunks, both)
    sum_layers(chunks - 1)

    def finish(step):
        position, chunk = visit(step)
        owner, index = split(chunk)

        @pl.when(owner == layer)
        def _():
            to_twin(chunk).wait_send()
            remote(rbuf.at[index], rbuf.at[index], r_send.at[index], r_recv.at[index],
                   "rows", twin).wait_recv()
            out[pl.ds(pl.multiple_of(index * height, height), height), :] = pbuf[chunk, side] + rbuf[index]

        @pl.when(owner != layer)
        def _():
            to_layer(chunk).wait_send()

        @pl.when((position >= place) & has_left)
        def _():
            forward(chunk, 0, left).wait_send()

        @pl.when((position <= place) & has_right)
        def _():
            forward(chunk, 1, right).wait_send()

    loop(0, chunks, finish)
    for part in range(parts):
        twin_query(part).wait_send()
    for piece in range(pieces):
        twin_train(piece).wait_send()


def solution(mesh):
    line, layers = mesh.shape["rows"] // 2, mesh.shape["layers"]

    def shards(train_grads, query_grads):
        train = train_grads.reshape(train_grads.shape[0], -1)
        queries = jnp.moveaxis(query_grads, 0, 1).reshape(query_grads.shape[1], -1)
        rows, depth = train.shape
        mine = queries.shape[0]
        every = mine * 2 * line
        share = every // layers
        height = math.gcd(math.gcd(mine, share), max(mine // PARTS, 64))
        parts, chunks, owned, half = mine // height, every // height, share // height, depth // 2
        pieces = PIECES if rows % (16 * PIECES) == 0 else 1
        dma = pltpu.SemaphoreType.DMA
        return pl.pallas_call(
            functools.partial(kernel, line, layers, parts),
            out_shape=jax.ShapeDtypeStruct((share, rows), jnp.float32),
            in_specs=[pl.BlockSpec(memory_space=pl.ANY)] * 2,
            out_specs=pl.BlockSpec(memory_space=pltpu.VMEM),
            scratch_shapes=[
                pltpu.VMEM((chunks, height, half), train.dtype),
                pltpu.VMEM((2, rows, half), train.dtype),
                pltpu.VMEM((chunks, 2, height, rows), jnp.float32),
                pltpu.VMEM((layers, owned, 2, height, rows), jnp.float32),
                pltpu.VMEM((owned, height, rows), jnp.float32),
                dma((chunks,)),
                dma((2, chunks)),
                dma((parts,)),
                dma((pieces + 1,)),
                dma((pieces,)),
                dma((layers, owned)),
                dma((chunks,)),
                dma((owned,)),
                dma((owned,)),
            ],
            compiler_params=pltpu.CompilerParams(
                collective_id=0, has_side_effects=True, vmem_limit_bytes=48 << 20),
            cost_estimate=pl.CostEstimate(
                flops=2 * every * rows * depth, transcendentals=0,
                bytes_accessed=2 * (rows + mine) * depth + 4 * share * rows),
        )(train, queries)

    in_specs = (P(("groups", "rows"), "layers", None), P("layers", ("groups", "rows"), None))
    out_specs = P("layers", ("groups", "rows"))
    return jax.shard_map(shards, mesh=mesh, in_specs=in_specs, out_specs=out_specs, check_vma=False)
```

```python
import functools
import math

import jax
import jax.numpy as jnp
from jax import lax
from jax.experimental import pallas as pl
from jax.experimental.pallas import tpu as pltpu
from jax.sharding import PartitionSpec as P

PARTS = 2
PIECES = 4
MESH = pl.DeviceIdType.MESH


def schedule(step, place, side, line, parts):
    subs = 2 * parts
    near = jnp.minimum(place, line - 1 - place)
    far = jnp.where(place < line - 1 - place, 1, -1)
    past = step - subs
    paired = past < 2 * near * subs
    within = lax.rem(past, 2 * subs)
    rest = past - 2 * near * subs
    apart = jnp.where(paired, past // (2 * subs) + 1, near + 1 + rest // subs)
    way = jnp.where(paired & (lax.rem(within, 2) == 1), -far, far)
    own = step < subs
    position = jnp.where(own, place, place + way * apart)
    turn = jnp.where(own, step, jnp.where(paired, within // 2, lax.rem(rest, subs)))
    shard = jnp.where(turn < parts, side, 1 - side)
    return position, shard, lax.rem(turn, parts)


def kernel(line, layers, parts, train, queries, out, qbuf, tbuf, pbuf, lbuf, rbuf,
           q_recv, q_send, x_send, t_recv, t_send, l_recv, l_send, r_recv, r_send):
    chunks, height, half = qbuf.shape
    rows = tbuf.shape[1]
    owned = rbuf.shape[0]
    subs = 2 * parts
    me = lax.axis_index("rows")
    layer = lax.axis_index("layers")
    place, side = me // 2, lax.rem(me, 2)
    other = 1 - side
    twin = me + 1 - 2 * side
    has_left, has_right = place > 0, place < line - 1
    left = jnp.where(has_left, me - 2, me)
    right = jnp.where(has_right, me + 2, me)
    pieces = t_recv.shape[0] - 1
    tall = rows // pieces
    mine = pl.ds(pl.multiple_of(side * half, half), half)
    theirs = pl.ds(pl.multiple_of(other * half, half), half)

    def name(position, shard, part):
        return (position * 2 + shard) * parts + part

    def visit(step):
        position, shard, part = schedule(step, place, side, line, parts)
        return position, name(position, shard, part)

    def remote(src, dst, send, recv, axis, device):
        return pltpu.make_async_remote_copy(
            src_ref=src, dst_ref=dst, send_sem=send, recv_sem=recv,
            device_id={axis: device}, device_id_type=MESH)

    def local_query(part):
        chunk = name(place, side, part)
        return pltpu.make_async_copy(
            queries.at[pl.ds(part * height, height), mine], qbuf.at[chunk], q_recv.at[chunk])

    def twin_query(part):
        chunk = name(place, side, part)
        return remote(queries.at[pl.ds(part * height, height), theirs], qbuf.at[chunk],
                      x_send.at[part], q_recv.at[chunk], "rows", twin)

    def own_query(part, way, device):
        chunk = name(place, side, part)
        return remote(queries.at[pl.ds(part * height, height), mine], qbuf.at[chunk],
                      q_send.at[way, chunk], q_recv.at[chunk], "rows", device)

    def forward(chunk, way, device):
        return remote(qbuf.at[chunk], qbuf.at[chunk], q_send.at[way, chunk], q_recv.at[chunk],
                      "rows", device)

    def twin_train(piece):
        return remote(train.at[pl.ds(piece * tall, tall), theirs],
                      tbuf.at[side, pl.ds(piece * tall, tall), :],
                      t_send.at[piece], t_recv.at[piece], "rows", twin)

    def local_train():
        return pltpu.make_async_copy(train.at[:, mine], tbuf.at[side], t_recv.at[pieces])

    def split(chunk):
        owner = chunk // owned
        return owner, chunk - owner * owned

    def to_layer(chunk):
        owner, index = split(chunk)
        return remote(pbuf.at[chunk], lbuf.at[layer, index], l_send.at[chunk],
                      l_recv.at[layer, index], "layers", owner)

    def to_twin(chunk):
        _, index = split(chunk)
        return remote(pbuf.at[chunk, other], rbuf.at[index], r_send.at[index], r_recv.at[index],
                      "rows", twin)

    barrier = pltpu.get_barrier_semaphore()
    pl.semaphore_signal(barrier, inc=1, device_id={"rows": twin}, device_id_type=MESH)

    @pl.when(has_left)
    def _():
        pl.semaphore_signal(barrier, inc=1, device_id={"rows": left}, device_id_type=MESH)

    @pl.when(has_right)
    def _():
        pl.semaphore_signal(barrier, inc=1, device_id={"rows": right}, device_id_type=MESH)

    for hop in range(1, layers):
        pl.semaphore_signal(barrier, inc=1, device_id={"layers": lax.rem(layer + hop, layers)},
                            device_id_type=MESH)
    for part in range(parts):
        local_query(part).start()
    local_train().start()
    pl.semaphore_wait(
        barrier, layers + has_left.astype(jnp.int32) + has_right.astype(jnp.int32))

    for part in range(parts):
        twin_query(part).start()

        @pl.when(has_left)
        def _():
            own_query(part, 0, left).start()

        @pl.when(has_right)
        def _():
            own_query(part, 1, right).start()

    def arrive(step):
        position, chunk = visit(step)
        own = step < parts
        forward(chunk, 0, twin).wait_recv()

        @pl.when((position >= place) & has_left & jnp.logical_not(own))
        def _():
            forward(chunk, 0, left).start()

        @pl.when((position <= place) & has_right & jnp.logical_not(own))
        def _():
            forward(chunk, 1, right).start()

    def loop(low, high, body):
        lax.fori_loop(low, high, lambda step, carry: (body(step), carry)[1], 0)

    loop(0, subs, arrive)
    for piece in range(pieces):
        twin_train(piece).start()
    inner = has_left & has_right
    loop(subs, jnp.where(inner, chunks, subs), arrive)
    local_train().wait()
    for piece in range(pieces):
        remote(tbuf.at[other, pl.ds(piece * tall, tall), :], tbuf.at[other, pl.ds(piece * tall, tall), :],
               t_send.at[piece], t_recv.at[piece], "rows", twin).wait_recv()

    def to_owner(chunk):
        owner, _ = split(chunk)

        @pl.when(owner != layer)
        def _():
            to_layer(chunk).start()

    def sum_layers(chunk):
        owner, index = split(chunk)

        @pl.when(owner == layer)
        def _():
            for hop in range(1, layers):
                source = lax.rem(layer + hop, layers)
                remote(pbuf.at[chunk], lbuf.at[source, index], l_send.at[chunk],
                       l_recv.at[source, index], "rows", twin).wait_recv()
                for shard in range(2):
                    pbuf[chunk, shard] = pbuf[chunk, shard] + lbuf[source, index, shard]
            to_twin(chunk).start()

    def product(first, count):
        block = qbuf[pl.ds(first, count)].reshape(count * height, half)
        for shard in range(2):
            terms = lax.dot_general(
                block, tbuf[shard], (((1,), (1,)), ((), ())), preferred_element_type=jnp.float32)
            pbuf[pl.ds(first, count), shard] = terms.reshape(count, height, rows)

    def first_of(turn):
        return subs * jnp.where(inner, turn, jnp.where(has_right, turn, line - 1 - turn))

    def position(turn):
        @pl.when(jnp.logical_not(inner) & (turn > 0))
        def _():
            loop(turn * subs, turn * subs + subs, arrive)

        product(first_of(turn), subs)
        for sub in range(subs):
            to_owner(first_of(turn) + sub)

        @pl.when(turn > 0)
        def _():
            for sub in range(subs):
                sum_layers(first_of(turn - 1) + sub)

    whole = jnp.where(inner, line, line - 1)
    loop(0, whole, position)
    for sub in range(subs):
        sum_layers(first_of(whole - 1) + sub)

    def last(step):
        arrive(step)
        _, chunk = visit(step)
        product(chunk, 1)
        to_owner(chunk)

        @pl.when(step > chunks - subs)
        def _():
            sum_layers(visit(step - 1)[1])

    def finish(step):
        position, chunk = visit(step)
        owner, index = split(chunk)

        @pl.when(owner == layer)
        def _():
            to_twin(chunk).wait_send()
            remote(rbuf.at[index], rbuf.at[index], r_send.at[index], r_recv.at[index],
                   "rows", twin).wait_recv()
            out[pl.ds(pl.multiple_of(index * height, height), height), :] = pbuf[chunk, side] + rbuf[index]

        @pl.when(owner != layer)
        def _():
            to_layer(chunk).wait_send()

        @pl.when((position >= place) & has_left)
        def _():
            forward(chunk, 0, left).wait_send()

        @pl.when((position <= place) & has_right)
        def _():
            forward(chunk, 1, right).wait_send()

    @pl.when(jnp.logical_not(inner))
    def _():
        loop(chunks - subs, chunks - parts, last)
        loop(0, chunks - subs, finish)
        loop(chunks - parts, chunks, last)
        sum_layers(visit(chunks - 1)[1])

    loop(jnp.where(inner, 0, chunks - subs), chunks, finish)
    for part in range(parts):
        twin_query(part).wait_send()
    for piece in range(pieces):
        twin_train(piece).wait_send()


def solution(mesh):
    line, layers = mesh.shape["rows"] // 2, mesh.shape["layers"]

    def shards(train_grads, query_grads):
        train = train_grads.reshape(train_grads.shape[0], -1)
        queries = jnp.moveaxis(query_grads, 0, 1).reshape(query_grads.shape[1], -1)
        rows, depth = train.shape
        mine = queries.shape[0]
        every = mine * 2 * line
        share = every // layers
        height = math.gcd(math.gcd(mine, share), max(mine // PARTS, 64))
        parts, chunks, owned, half = mine // height, every // height, share // height, depth // 2
        pieces = PIECES if rows % (16 * PIECES) == 0 else 1
        dma = pltpu.SemaphoreType.DMA
        return pl.pallas_call(
            functools.partial(kernel, line, layers, parts),
            out_shape=jax.ShapeDtypeStruct((share, rows), jnp.float32),
            in_specs=[pl.BlockSpec(memory_space=pl.ANY)] * 2,
            out_specs=pl.BlockSpec(memory_space=pltpu.VMEM),
            scratch_shapes=[
                pltpu.VMEM((chunks, height, half), train.dtype),
                pltpu.VMEM((2, rows, half), train.dtype),
                pltpu.VMEM((chunks, 2, height, rows), jnp.float32),
                pltpu.VMEM((layers, owned, 2, height, rows), jnp.float32),
                pltpu.VMEM((owned, height, rows), jnp.float32),
                dma((chunks,)),
                dma((2, chunks)),
                dma((parts,)),
                dma((pieces + 1,)),
                dma((pieces,)),
                dma((layers, owned)),
                dma((chunks,)),
                dma((owned,)),
                dma((owned,)),
            ],
            compiler_params=pltpu.CompilerParams(
                collective_id=0, has_side_effects=True, vmem_limit_bytes=55000000),
            cost_estimate=pl.CostEstimate(
                flops=2 * every * rows * depth, transcendentals=0,
                bytes_accessed=2 * (rows + mine) * depth + 4 * share * rows),
        )(train, queries)

    in_specs = (P(("groups", "rows"), "layers", None), P("layers", ("groups", "rows"), None))
    out_specs = P("layers", ("groups", "rows"))
    return jax.shard_map(shards, mesh=mesh, in_specs=in_specs, out_specs=out_specs, check_vma=False)
```

```python
import functools
import math

import jax
import jax.numpy as jnp
from jax import lax
from jax.experimental import pallas as pl
from jax.experimental.pallas import tpu as pltpu
from jax.sharding import PartitionSpec as P

PARTS = 2
PIECES = 4
MESH = pl.DeviceIdType.MESH


def schedule(step, place, side, line, parts):
    subs = 2 * parts
    near = jnp.minimum(place, line - 1 - place)
    far = jnp.where(place < line - 1 - place, 1, -1)
    past = step - subs
    paired = past < 2 * near * subs
    within = lax.rem(past, 2 * subs)
    rest = past - 2 * near * subs
    apart = jnp.where(paired, past // (2 * subs) + 1, near + 1 + rest // subs)
    way = jnp.where(paired & (lax.rem(within, 2) == 1), -far, far)
    own = step < subs
    position = jnp.where(own, place, place + way * apart)
    turn = jnp.where(own, step, jnp.where(paired, within // 2, lax.rem(rest, subs)))
    shard = jnp.where(turn < parts, side, 1 - side)
    return position, shard, lax.rem(turn, parts)


def kernel(line, layers, parts, train, queries, out, qbuf, tbuf, pbuf, lbuf, rbuf,
           q_recv, q_send, x_send, t_recv, t_send, l_recv, l_send, r_recv, r_send):
    chunks, height, half = qbuf.shape
    rows = tbuf.shape[1]
    owned = rbuf.shape[0]
    subs = 2 * parts
    me = lax.axis_index("rows")
    layer = lax.axis_index("layers")
    place, side = me // 2, lax.rem(me, 2)
    other = 1 - side
    turns = (other, side)
    twin = me + 1 - 2 * side
    has_left, has_right = place > 0, place < line - 1
    left = jnp.where(has_left, me - 2, me)
    right = jnp.where(has_right, me + 2, me)
    pieces = t_recv.shape[0] - 1
    tall = rows // pieces
    mine = pl.ds(pl.multiple_of(side * half, half), half)
    theirs = pl.ds(pl.multiple_of(other * half, half), half)

    def name(position, shard, part):
        return (position * 2 + shard) * parts + part

    def visit(step):
        position, shard, part = schedule(step, place, side, line, parts)
        return position, name(position, shard, part)

    def remote(src, dst, send, recv, axis, device):
        return pltpu.make_async_remote_copy(
            src_ref=src, dst_ref=dst, send_sem=send, recv_sem=recv,
            device_id={axis: device}, device_id_type=MESH)

    def local_query(part):
        chunk = name(place, side, part)
        return pltpu.make_async_copy(
            queries.at[pl.ds(part * height, height), mine], qbuf.at[chunk], q_recv.at[chunk])

    def twin_query(part):
        chunk = name(place, side, part)
        return remote(queries.at[pl.ds(part * height, height), theirs], qbuf.at[chunk],
                      x_send.at[part], q_recv.at[chunk], "rows", twin)

    def own_query(part, way, device):
        chunk = name(place, side, part)
        return remote(queries.at[pl.ds(part * height, height), mine], qbuf.at[chunk],
                      q_send.at[way, chunk], q_recv.at[chunk], "rows", device)

    def forward(chunk, way, device):
        return remote(qbuf.at[chunk], qbuf.at[chunk], q_send.at[way, chunk], q_recv.at[chunk],
                      "rows", device)

    def twin_train(piece):
        return remote(train.at[pl.ds(piece * tall, tall), theirs],
                      tbuf.at[side, pl.ds(piece * tall, tall), :],
                      t_send.at[piece], t_recv.at[piece], "rows", twin)

    def local_train():
        return pltpu.make_async_copy(train.at[:, mine], tbuf.at[side], t_recv.at[pieces])

    def split(chunk):
        owner = chunk // owned
        return owner, chunk - owner * owned

    def to_layer(chunk, turn):
        owner, index = split(chunk)
        shard = turns[turn]
        return remote(pbuf.at[chunk, shard], lbuf.at[layer, index, shard], l_send.at[turn, chunk],
                      l_recv.at[turn, layer, index], "layers", owner)

    def to_twin(chunk):
        _, index = split(chunk)
        return remote(pbuf.at[chunk, other], rbuf.at[index], r_send.at[index], r_recv.at[index],
                      "rows", twin)

    barrier = pltpu.get_barrier_semaphore()
    pl.semaphore_signal(barrier, inc=1, device_id={"rows": twin}, device_id_type=MESH)

    @pl.when(has_left)
    def _():
        pl.semaphore_signal(barrier, inc=1, device_id={"rows": left}, device_id_type=MESH)

    @pl.when(has_right)
    def _():
        pl.semaphore_signal(barrier, inc=1, device_id={"rows": right}, device_id_type=MESH)

    for hop in range(1, layers):
        pl.semaphore_signal(barrier, inc=1, device_id={"layers": lax.rem(layer + hop, layers)},
                            device_id_type=MESH)
    for part in range(parts):
        local_query(part).start()
    local_train().start()
    pl.semaphore_wait(
        barrier, layers + has_left.astype(jnp.int32) + has_right.astype(jnp.int32))

    for part in range(parts):
        twin_query(part).start()

        @pl.when(has_left)
        def _():
            own_query(part, 0, left).start()

        @pl.when(has_right)
        def _():
            own_query(part, 1, right).start()

    def arrive(step):
        position, chunk = visit(step)
        own = step < parts
        forward(chunk, 0, twin).wait_recv()

        @pl.when((position >= place) & has_left & jnp.logical_not(own))
        def _():
            forward(chunk, 0, left).start()

        @pl.when((position <= place) & has_right & jnp.logical_not(own))
        def _():
            forward(chunk, 1, right).start()

    def loop(low, high, body):
        lax.fori_loop(low, high, lambda step, carry: (body(step), carry)[1], 0)

    loop(0, subs, arrive)
    for piece in range(pieces):
        twin_train(piece).start()
    inner = has_left & has_right
    loop(subs, jnp.where(inner, chunks, subs), arrive)
    local_train().wait()
    for piece in range(pieces):
        remote(tbuf.at[other, pl.ds(piece * tall, tall), :], tbuf.at[other, pl.ds(piece * tall, tall), :],
               t_send.at[piece], t_recv.at[piece], "rows", twin).wait_recv()

    def sum_layers(chunk):
        owner, index = split(chunk)

        @pl.when(owner == layer)
        def _():
            for turn, shard in enumerate(turns):
                for hop in range(1, layers):
                    source = lax.rem(layer + hop, layers)
                    remote(pbuf.at[chunk, shard], lbuf.at[source, index, shard], l_send.at[turn, chunk],
                           l_recv.at[turn, source, index], "rows", twin).wait_recv()
                    pbuf[chunk, shard] = pbuf[chunk, shard] + lbuf[source, index, shard]
                if turn == 0:
                    to_twin(chunk).start()

    def product(first, count):
        block = qbuf[pl.ds(first, count)].reshape(count * height, half)
        for turn, shard in enumerate(turns):
            terms = lax.dot_general(
                block, tbuf[shard], (((1,), (1,)), ((), ())), preferred_element_type=jnp.float32)
            pbuf[pl.ds(first, count), shard] = terms.reshape(count, height, rows)
            for sub in range(count):
                owner, _ = split(first + sub)

                @pl.when(owner != layer)
                def _():
                    to_layer(first + sub, turn).start()

    def first_of(turn):
        return subs * jnp.where(inner, turn, jnp.where(has_right, turn, line - 1 - turn))

    def position(turn):
        @pl.when(jnp.logical_not(inner) & (turn > 0))
        def _():
            loop(turn * subs, turn * subs + subs, arrive)

        product(first_of(turn), subs)

        @pl.when(turn > 0)
        def _():
            for sub in range(subs):
                sum_layers(first_of(turn - 1) + sub)

    whole = jnp.where(inner, line, line - 1)
    loop(0, whole, position)
    for sub in range(subs):
        sum_layers(first_of(whole - 1) + sub)

    def last(step):
        arrive(step)
        _, chunk = visit(step)
        product(chunk, 1)

        @pl.when(step > chunks - subs)
        def _():
            sum_layers(visit(step - 1)[1])

    def finish(step):
        position, chunk = visit(step)
        owner, index = split(chunk)

        @pl.when(owner == layer)
        def _():
            to_twin(chunk).wait_send()
            remote(rbuf.at[index], rbuf.at[index], r_send.at[index], r_recv.at[index],
                   "rows", twin).wait_recv()
            out[pl.ds(pl.multiple_of(index * height, height), height), :] = pbuf[chunk, side] + rbuf[index]

        @pl.when(owner != layer)
        def _():
            for turn in range(2):
                to_layer(chunk, turn).wait_send()

        @pl.when((position >= place) & has_left)
        def _():
            forward(chunk, 0, left).wait_send()

        @pl.when((position <= place) & has_right)
        def _():
            forward(chunk, 1, right).wait_send()

    @pl.when(jnp.logical_not(inner))
    def _():
        loop(chunks - subs, chunks - parts, last)
        loop(0, chunks - subs, finish)
        loop(chunks - parts, chunks, last)
        sum_layers(visit(chunks - 1)[1])

    loop(jnp.where(inner, 0, chunks - subs), chunks, finish)
    for part in range(parts):
        twin_query(part).wait_send()
    for piece in range(pieces):
        twin_train(piece).wait_send()


def solution(mesh):
    line, layers = mesh.shape["rows"] // 2, mesh.shape["layers"]

    def shards(train_grads, query_grads):
        train = train_grads.reshape(train_grads.shape[0], -1)
        queries = jnp.moveaxis(query_grads, 0, 1).reshape(query_grads.shape[1], -1)
        rows, depth = train.shape
        mine = queries.shape[0]
        every = mine * 2 * line
        share = every // layers
        height = math.gcd(math.gcd(mine, share), max(mine // PARTS, 64))
        parts, chunks, owned, half = mine // height, every // height, share // height, depth // 2
        pieces = PIECES if rows % (16 * PIECES) == 0 else 1
        dma = pltpu.SemaphoreType.DMA
        return pl.pallas_call(
            functools.partial(kernel, line, layers, parts),
            out_shape=jax.ShapeDtypeStruct((share, rows), jnp.float32),
            in_specs=[pl.BlockSpec(memory_space=pl.ANY)] * 2,
            out_specs=pl.BlockSpec(memory_space=pltpu.VMEM),
            scratch_shapes=[
                pltpu.VMEM((chunks, height, half), train.dtype),
                pltpu.VMEM((2, rows, half), train.dtype),
                pltpu.VMEM((chunks, 2, height, rows), jnp.float32),
                pltpu.VMEM((layers, owned, 2, height, rows), jnp.float32),
                pltpu.VMEM((owned, height, rows), jnp.float32),
                dma((chunks,)),
                dma((2, chunks)),
                dma((parts,)),
                dma((pieces + 1,)),
                dma((pieces,)),
                dma((2, layers, owned)),
                dma((2, chunks)),
                dma((owned,)),
                dma((owned,)),
            ],
            compiler_params=pltpu.CompilerParams(
                collective_id=0, has_side_effects=True, vmem_limit_bytes=55000000),
            cost_estimate=pl.CostEstimate(
                flops=2 * every * rows * depth, transcendentals=0,
                bytes_accessed=2 * (rows + mine) * depth + 4 * share * rows),
        )(train, queries)

    in_specs = (P(("groups", "rows"), "layers", None), P("layers", ("groups", "rows"), None))
    out_specs = P("layers", ("groups", "rows"))
    return jax.shard_map(shards, mesh=mesh, in_specs=in_specs, out_specs=out_specs, check_vma=False)
```

```python
import functools
import math

import jax
import jax.numpy as jnp
from jax import lax
from jax.experimental import pallas as pl
from jax.experimental.pallas import tpu as pltpu
from jax.sharding import PartitionSpec as P

PARTS = 2
PIECES = 1
MESH = pl.DeviceIdType.MESH


def schedule(step, place, side, line, parts):
    subs = 2 * parts
    near = jnp.minimum(place, line - 1 - place)
    far = jnp.where(place < line - 1 - place, 1, -1)
    past = step - subs
    paired = past < 2 * near * subs
    within = lax.rem(past, 2 * subs)
    rest = past - 2 * near * subs
    apart = jnp.where(paired, past // (2 * subs) + 1, near + 1 + rest // subs)
    way = jnp.where(paired & (lax.rem(within, 2) == 1), -far, far)
    own = step < subs
    position = jnp.where(own, place, place + way * apart)
    turn = jnp.where(own, step, jnp.where(paired, within // 2, lax.rem(rest, subs)))
    shard = jnp.where(turn < parts, side, 1 - side)
    return position, shard, lax.rem(turn, parts)


def kernel(line, layers, parts, train, queries, out, qbuf, tbuf, pbuf, lbuf, rbuf,
           q_recv, q_send, x_send, t_recv, t_send, l_recv, l_send, r_recv, r_send):
    chunks, height, half = qbuf.shape
    rows = tbuf.shape[1]
    owned = rbuf.shape[0]
    subs = 2 * parts
    me = lax.axis_index("rows")
    layer = lax.axis_index("layers")
    place, side = me // 2, lax.rem(me, 2)
    other = 1 - side
    turns = (other, side)
    twin = me + 1 - 2 * side
    has_left, has_right = place > 0, place < line - 1
    left = jnp.where(has_left, me - 2, me)
    right = jnp.where(has_right, me + 2, me)
    pieces = t_recv.shape[0] - 1
    tall = rows // pieces
    mine = pl.ds(pl.multiple_of(side * half, half), half)
    theirs = pl.ds(pl.multiple_of(other * half, half), half)

    def name(position, shard, part):
        return (position * 2 + shard) * parts + part

    def visit(step):
        position, shard, part = schedule(step, place, side, line, parts)
        return position, name(position, shard, part)

    def remote(src, dst, send, recv, axis, device):
        return pltpu.make_async_remote_copy(
            src_ref=src, dst_ref=dst, send_sem=send, recv_sem=recv,
            device_id={axis: device}, device_id_type=MESH)

    def local_query(part):
        chunk = name(place, side, part)
        return pltpu.make_async_copy(
            queries.at[pl.ds(part * height, height), mine], qbuf.at[chunk], q_recv.at[chunk])

    def twin_query(part):
        chunk = name(place, side, part)
        return remote(queries.at[pl.ds(part * height, height), theirs], qbuf.at[chunk],
                      x_send.at[part], q_recv.at[chunk], "rows", twin)

    def own_query(part, way, device):
        chunk = name(place, side, part)
        return remote(queries.at[pl.ds(part * height, height), mine], qbuf.at[chunk],
                      q_send.at[way, chunk], q_recv.at[chunk], "rows", device)

    def forward(chunk, way, device):
        return remote(qbuf.at[chunk], qbuf.at[chunk], q_send.at[way, chunk], q_recv.at[chunk],
                      "rows", device)

    def twin_train(piece):
        return remote(train.at[pl.ds(piece * tall, tall), theirs],
                      tbuf.at[side, pl.ds(piece * tall, tall), :],
                      t_send.at[piece], t_recv.at[piece], "rows", twin)

    def local_train():
        return pltpu.make_async_copy(train.at[:, mine], tbuf.at[side], t_recv.at[pieces])

    def split(chunk):
        owner = chunk // owned
        return owner, chunk - owner * owned

    def to_layer(chunk, turn):
        owner, index = split(chunk)
        shard = turns[turn]
        return remote(pbuf.at[chunk, shard], lbuf.at[layer, index, shard], l_send.at[turn, chunk],
                      l_recv.at[turn, layer, index], "layers", owner)

    def to_twin(chunk):
        _, index = split(chunk)
        return remote(pbuf.at[chunk, other], rbuf.at[index], r_send.at[index], r_recv.at[index],
                      "rows", twin)

    barrier = pltpu.get_barrier_semaphore()
    pl.semaphore_signal(barrier, inc=1, device_id={"rows": twin}, device_id_type=MESH)

    @pl.when(has_left)
    def _():
        pl.semaphore_signal(barrier, inc=1, device_id={"rows": left}, device_id_type=MESH)

    @pl.when(has_right)
    def _():
        pl.semaphore_signal(barrier, inc=1, device_id={"rows": right}, device_id_type=MESH)

    for hop in range(1, layers):
        pl.semaphore_signal(barrier, inc=1, device_id={"layers": lax.rem(layer + hop, layers)},
                            device_id_type=MESH)
    for part in range(parts):
        local_query(part).start()
    local_train().start()
    pl.semaphore_wait(
        barrier, layers + has_left.astype(jnp.int32) + has_right.astype(jnp.int32))

    for part in range(parts):
        @pl.when(has_left)
        def _():
            own_query(part, 0, left).start()

        @pl.when(has_right)
        def _():
            own_query(part, 1, right).start()

        twin_query(part).start()

    def arrive(step):
        position, chunk = visit(step)
        own = step < parts
        forward(chunk, 0, twin).wait_recv()

        @pl.when((position >= place) & has_left & jnp.logical_not(own))
        def _():
            forward(chunk, 0, left).start()

        @pl.when((position <= place) & has_right & jnp.logical_not(own))
        def _():
            forward(chunk, 1, right).start()

    def loop(low, high, body):
        lax.fori_loop(low, high, lambda step, carry: (body(step), carry)[1], 0)

    loop(0, subs, arrive)
    for piece in range(pieces):
        twin_train(piece).start()
    inner = has_left & has_right
    loop(subs, jnp.where(inner, chunks, subs), arrive)
    local_train().wait()
    for piece in range(pieces):
        remote(tbuf.at[other, pl.ds(piece * tall, tall), :], tbuf.at[other, pl.ds(piece * tall, tall), :],
               t_send.at[piece], t_recv.at[piece], "rows", twin).wait_recv()

    def sum_layers(chunk):
        owner, index = split(chunk)

        @pl.when(owner == layer)
        def _():
            for turn, shard in enumerate(turns):
                for hop in range(1, layers):
                    source = lax.rem(layer + hop, layers)
                    remote(pbuf.at[chunk, shard], lbuf.at[source, index, shard], l_send.at[turn, chunk],
                           l_recv.at[turn, source, index], "rows", twin).wait_recv()
                    pbuf[chunk, shard] = pbuf[chunk, shard] + lbuf[source, index, shard]
                if turn == 0:
                    to_twin(chunk).start()

    def product(first, count):
        block = qbuf[pl.ds(first, count)].reshape(count * height, half)
        for turn, shard in enumerate(turns):
            terms = lax.dot_general(
                block, tbuf[shard], (((1,), (1,)), ((), ())), preferred_element_type=jnp.float32)
            pbuf[pl.ds(first, count), shard] = terms.reshape(count, height, rows)
            for sub in range(count):
                owner, _ = split(first + sub)

                @pl.when(owner != layer)
                def _():
                    to_layer(first + sub, turn).start()

    def first_of(turn):
        return subs * jnp.where(inner, turn, jnp.where(has_right, turn, line - 1 - turn))

    def position(turn):
        @pl.when(jnp.logical_not(inner) & (turn > 0))
        def _():
            loop(turn * subs, turn * subs + subs, arrive)

        product(first_of(turn), subs)

        @pl.when(turn > 0)
        def _():
            for sub in range(subs):
                sum_layers(first_of(turn - 1) + sub)

    whole = jnp.where(inner, line, line - 1)
    loop(0, whole, position)
    for sub in range(subs):
        sum_layers(first_of(whole - 1) + sub)

    def last(step):
        arrive(step)
        _, chunk = visit(step)
        product(chunk, 1)

        @pl.when(step > chunks - subs)
        def _():
            sum_layers(visit(step - 1)[1])

    def finish(step):
        position, chunk = visit(step)
        owner, index = split(chunk)

        @pl.when(owner == layer)
        def _():
            to_twin(chunk).wait_send()
            remote(rbuf.at[index], rbuf.at[index], r_send.at[index], r_recv.at[index],
                   "rows", twin).wait_recv()
            out[pl.ds(pl.multiple_of(index * height, height), height), :] = pbuf[chunk, side] + rbuf[index]

        @pl.when(owner != layer)
        def _():
            for turn in range(2):
                to_layer(chunk, turn).wait_send()

        @pl.when((position >= place) & has_left)
        def _():
            forward(chunk, 0, left).wait_send()

        @pl.when((position <= place) & has_right)
        def _():
            forward(chunk, 1, right).wait_send()

    @pl.when(jnp.logical_not(inner))
    def _():
        loop(chunks - subs, chunks - parts, last)
        loop(0, chunks - subs, finish)
        loop(chunks - parts, chunks, last)
        sum_layers(visit(chunks - 1)[1])

    loop(jnp.where(inner, 0, chunks - subs), chunks, finish)
    for part in range(parts):
        twin_query(part).wait_send()
    for piece in range(pieces):
        twin_train(piece).wait_send()


def solution(mesh):
    line, layers = mesh.shape["rows"] // 2, mesh.shape["layers"]

    def shards(train_grads, query_grads):
        train = train_grads.reshape(train_grads.shape[0], -1)
        queries = jnp.moveaxis(query_grads, 0, 1).reshape(query_grads.shape[1], -1)
        rows, depth = train.shape
        mine = queries.shape[0]
        every = mine * 2 * line
        share = every // layers
        height = math.gcd(math.gcd(mine, share), max(mine // PARTS, 64))
        parts, chunks, owned, half = mine // height, every // height, share // height, depth // 2
        pieces = PIECES if rows % (16 * PIECES) == 0 else 1
        dma = pltpu.SemaphoreType.DMA
        return pl.pallas_call(
            functools.partial(kernel, line, layers, parts),
            out_shape=jax.ShapeDtypeStruct((share, rows), jnp.float32),
            in_specs=[pl.BlockSpec(memory_space=pl.ANY)] * 2,
            out_specs=pl.BlockSpec(memory_space=pltpu.VMEM),
            scratch_shapes=[
                pltpu.VMEM((chunks, height, half), train.dtype),
                pltpu.VMEM((2, rows, half), train.dtype),
                pltpu.VMEM((chunks, 2, height, rows), jnp.float32),
                pltpu.VMEM((layers, owned, 2, height, rows), jnp.float32),
                pltpu.VMEM((owned, height, rows), jnp.float32),
                dma((chunks,)),
                dma((2, chunks)),
                dma((parts,)),
                dma((pieces + 1,)),
                dma((pieces,)),
                dma((2, layers, owned)),
                dma((2, chunks)),
                dma((owned,)),
                dma((owned,)),
            ],
            compiler_params=pltpu.CompilerParams(
                collective_id=0, has_side_effects=True, vmem_limit_bytes=55000000),
            cost_estimate=pl.CostEstimate(
                flops=2 * every * rows * depth, transcendentals=0,
                bytes_accessed=2 * (rows + mine) * depth + 4 * share * rows),
        )(train, queries)

    in_specs = (P(("groups", "rows"), "layers", None), P("layers", ("groups", "rows"), None))
    out_specs = P("layers", ("groups", "rows"))
    return jax.shard_map(shards, mesh=mesh, in_specs=in_specs, out_specs=out_specs, check_vma=False)
```
